256 devices in a mesh: row: 8 (over y_lo, x), col: 32 (over z, y_hi, core).
Axes of the slice: x: 4, y: 4 (y_hi: 2, y_lo: 2; y = y_hi * 2 + y_lo), z: 8, core: 2. Of those that a mesh axis runs over, the one named last changes fastest.
Arguments:
- iterate: bfloat16 [3584, 16384], P('row', 'col'), may hold values from -0.0390625 to 0.0390625
Outputs:
- update: bfloat16 [3584, 16384], P('row', 'col')
The draws below stay inside these ranges and needn't reach their ends.
All inputs are finite; a program needn't handle non-finite values.
Results may differ from the reference program's by a relative error of at most 0.0087.
Values may be sent and summed in bfloat16 or wider, within the bound.
A program may use at most 64 MiB of HBM per device.

```python
import math
import jax
import jax.numpy as jnp

M = 3584
N = 16384


def levels(stream_key, extent, split, least, high):
    def one(axis_at, parts):
        draws = jax.random.uniform(jax.random.fold_in(jax.random.fold_in(stream_key, 6), axis_at), (parts,), jnp.float32, least / len(split), high / len(split))
        return jnp.repeat(jnp.exp(draws), extent[axis_at] // parts).reshape((-1,) + (1,) * (len(extent) - axis_at - 1))

    gain = one(*split[0])
    for cut in split[1:]:
        gain = gain * one(*cut)
    return gain


def normal_values(key, extent, spread, reach, pieces=(), kind=jnp.bfloat16):
    entries = jax.random.normal(key, extent, jnp.float32) * spread
    if len(pieces) > 0:
        entries = levels(key, extent, pieces, -0.22, 0.18) * entries
    return jnp.clip(entries, min=-reach, max=reach).astype(kind)


def setup_inputs(seed: int = 0) -> dict:
    key_list = jax.random.split(jax.random.key(seed), 2)
    return {
        "iterate": normal_values(key_list[0], (M, N), (5 * N // 4) ** -0.5, 0.0390625, ((0, 8), (1, 32))),
    }


def reference(iterate):
    gram = jnp.dot(iterate, iterate.T, preferred_element_type=jnp.float32).astype(jnp.bfloat16)
    square = jnp.dot(gram, gram, preferred_element_type=jnp.float32)
    poly = (-4.775 * gram.astype(jnp.float32) + 2.0315 * square).astype(jnp.bfloat16)
    product = jnp.dot(poly, iterate, preferred_element_type=jnp.float32)
    scale = math.sqrt(N)
    return ((3.4445 * iterate.astype(jnp.float32) + product) * scale).astype(jnp.bfloat16)
```

```python
import math

import jax
import jax.numpy as jnp
from jax import lax
from jax.experimental import pallas as pl
from jax.experimental.pallas import tpu as pltpu
from jax.sharding import PartitionSpec as P

N = 16384
B = 448
W = 512
NX = 4
HALF = NX * B
NQ = 2
Q = W // NQ
HW = HALF // 2
CH = B // 4
SH = 64
F32 = jnp.float32
BF16 = jnp.bfloat16
NT = (((1,), (1,)), ((), ()))
PIECES = ((0, 256), (256, 256), (512, 256), (768, 128))


def kernel(
    x_ref, out_ref, panel, ypanel, tsend, town, ybuf, zsrc, zbuf, agbuf, poly,
    part, rbuf, yown, loc_sem, xs, xr, cs, cr, ls, lr, ys, yr, zs, zr, gs, gr, hs, hr,
    ps, pr,
):
    row = lax.axis_index("row")
    col = lax.axis_index("col")
    x = row % 4
    low = row // 4
    core = col % 2
    high = (col // 2) % 2
    z = col // 4

    def at(x_=None, low_=None, z_=None, high_=None, core_=None):
        x_ = x if x_ is None else x_
        low_ = low if low_ is None else low_
        z_ = z if z_ is None else z_
        high_ = high if high_ is None else high_
        core_ = core if core_ is None else core_
        return (low_ * 4 + x_, z_ * 4 + high_ * 2 + core_)

    def remote(src, dst, send, recv, dev):
        return pltpu.make_async_remote_copy(
            src_ref=src, dst_ref=dst, send_sem=send, recv_sem=recv,
            device_id=dev, device_id_type=pl.DeviceIdType.MESH,
        )

    up = at(x_=(x + 1) % 4)
    down = at(x_=(x + 3) % 4)
    twin = at(core_=1 - core)
    across = at(high_=1 - high)

    barrier = pltpu.get_barrier_semaphore()
    peers = [up, down, twin, across]
    peers += [at(low_=1 - low, core_=k) for k in range(2)]
    peers += [at(z_=(z + d) % 8) for d in range(1, 8)]
    for dev in peers:
        pl.semaphore_signal(barrier, inc=1, device_id=dev, device_id_type=pl.DeviceIdType.MESH)
    pl.semaphore_wait(barrier, len(peers))

    h = B // 2

    def gather(src, slot, n):
        own = src
        a, b = pl.ds(0, h), pl.ds(h, h)
        first = [
            remote(own.at[a], slot(core, B, h), xs.at[n, 0], xr.at[n, 0], down),
            remote(own.at[b], slot(core, 3 * B + h, h), xs.at[n, 1], xr.at[n, 1], up),
            remote(own.at[b], slot(core, B + h, h), xs.at[n, 2], xr.at[n, 2], down),
            remote(own.at[a], slot(core, 3 * B, h), xs.at[n, 3], xr.at[n, 3], up),
        ]
        passed = [
            remote(slot(core, B, h), slot(core, 2 * B, h), xs.at[n, 4], xr.at[n, 4], down),
            remote(slot(core, 3 * B + h, h), slot(core, 2 * B + h, h), xs.at[n, 5], xr.at[n, 5], up),
        ]
        places = [B, 3 * B + h, B + h, 3 * B, 2 * B, 2 * B + h]
        cross = [
            remote(slot(core, p, h), slot(core, p, h), cs.at[n, k], cr.at[n, k], twin)
            for k, p in enumerate(places)
        ]
        cross.append(remote(own, slot(core, 0, B), cs.at[n, 6], cr.at[n, 6], twin))

        def start():
            for c in first:
                c.start()
            cross[6].start()

        def relay():
            for k in range(6):
                (first + passed)[k].wait_recv()
                if k < 2:
                    passed[k].start()
                cross[k].start()

        def done():
            for c in cross:
                c.wait_recv()

        def close():
            for c in first + passed + cross:
                c.wait_send()

        return start, relay, done, close

    def xslot(c, at_row, rows):
        return panel.at[c, pl.ds(at_row, rows)]

    start, relay, done, close = gather(x_ref, xslot, 0)
    start()
    other = remote(
        x_ref, panel.at[core, pl.ds(HALF, B)], ls.at[0], lr.at[core], at(low_=1 - low, core_=1)
    )
    other.start()
    keep = pltpu.make_async_copy(x_ref, panel.at[core, pl.ds(0, B)], loc_sem)
    keep.start()
    relay()
    keep.wait()
    done()

    @pl.when(core == 1)
    def _():
        for k in range(2):
            remote(
                x_ref, panel.at[k, pl.ds(HALF, B)], ls.at[0], lr.at[k], at(low_=1 - low, core_=1)
            ).wait_recv()

    left = pl.multiple_of(core * HALF, 64)

    def gram(base, at_col, size):
        total = None
        for c in range(2):
            rows = pl.ds(pl.multiple_of(base + at_col, 64), size)
            term = lax.dot_general(
                panel[c, pl.ds(left, B), :], panel[c, rows, :], NT, preferred_element_type=F32
            )
            total = term if total is None else total + term
        return total

    for at_col, size in PIECES:
        tsend[:, at_col : at_col + size] = gram((1 - high) * HW, at_col, size).astype(BF16)
    i0 = z // 2
    ysend = []
    for s in range(4):
        rows = pl.ds(pl.multiple_of((i0 + s) % 4 * CH, 16), CH)
        ysend.append(remote(tsend.at[rows], ybuf.at[rows], ys.at[s], yr.at[s], across))
        ysend[s].start()
    for at_col, size in PIECES:
        town[:, at_col : at_col + size] = gram(high * HW, at_col, size)

    par = z % 2
    zsend = []
    for s in range(4):
        chunk = (i0 + s) % 4
        rows = pl.ds(pl.multiple_of(chunk * CH, 16), CH)
        ysend[s].wait_recv()
        zsrc[rows, :] = (town[rows, :] + ybuf[rows, :].astype(F32)).astype(BF16)
        if s == 0:
            odd = 1 - par
            piece = pl.ds(pl.multiple_of(chunk * CH + odd * (CH - SH), 16), SH)
            zsend.append(
                remote(zsrc.at[piece], zbuf.at[0], zs.at[0], zr.at[0], at(z_=2 * chunk + odd))
            )
            zsend[-1].start()
        else:
            for odd in range(2):
                piece = pl.ds(pl.multiple_of(chunk * CH + odd * (CH - SH), 16), SH)
                k = 2 * s - 1 + par
                zsend.append(
                    remote(
                        zsrc.at[piece], zbuf.at[k], zs.at[2 * s - 1 + odd], zr.at[k],
                        at(z_=2 * chunk + odd),
                    )
                )
                zsend[-1].start()
    mine = pl.ds(pl.multiple_of(i0 * CH + par * (CH - SH), 16), SH)
    total = zsrc[mine, :].astype(F32)
    for k in range(7):
        remote(zbuf.at[k], zbuf.at[k], zs.at[k], zr.at[k], at(z_=(z + 1) % 8)).wait_recv()
        total = total + zbuf[k].astype(F32)
    agbuf[0, 7] = total.astype(BF16)

    gsend = []
    for s in range(4):
        chunk = (i0 + s) % 4
        for odd in range(2) if s else (1 - par,):
            k = 2 * s - 1 + par if s else 0
            gsend.append(
                remote(
                    agbuf.at[0, 7], agbuf.at[0, k], gs.at[len(gsend)], gr.at[k],
                    at(z_=2 * chunk + odd),
                )
            )
            gsend[-1].start()
    hsend = [remote(agbuf.at[0, k], agbuf.at[1, k], hs.at[k], hr.at[k], across) for k in range(8)]
    hsend[7].start()

    def first_row(k):
        if k == 7:
            return i0 * CH + par * (CH - SH)
        if k == 0:
            return i0 * CH + (1 - par) * (CH - SH)
        s, odd = (k + 1) // 2, (k + 1) % 2
        return (i0 + 4 - s) % 4 * CH + odd * (CH - SH)

    def place(side, k):
        rows = pl.ds(pl.multiple_of(first_row(k), 16), SH)
        half = high if side == 0 else 1 - high
        poly[rows, pl.ds(pl.multiple_of(half * HW, 128), HW)] = agbuf[side, k]

    place(0, 7)
    for k in range(7):
        remote(agbuf.at[0, k], agbuf.at[0, k], gs.at[k], gr.at[k], at(z_=(z + 1) % 8)).wait_recv()
        hsend[k].start()
        place(0, k)
    for k in (7, 0, 1, 2, 3, 4, 5, 6):
        hsend[k].wait_recv()
        place(1, k)

    def send_partial(n, q):
        one = remote(
            part.at[n, q, 1], rbuf.at[n, q, core], ps.at[n, q, 1], pr.at[n, q, core],
            (row + core * (4 - 8 * low), z * 4 + high * 2 + 1),
        )
        one.start()

        @pl.when(core == 1)
        def _():
            remote(
                part.at[n, q, 0], rbuf.at[n, q, 1], ps.at[n, q, 0], pr.at[n, q, 1],
                at(low_=1 - low, core_=0),
            ).start()

    def reduced(n, q):
        remote(
            part.at[n, q, 1], rbuf.at[n, q, 1], ps.at[n, q, 1], pr.at[n, q, 1], twin
        ).wait_recv()

        @pl.when(core == 1)
        def _():
            remote(
                part.at[n, q, 0], rbuf.at[n, q, 0], ps.at[n, q, 0], pr.at[n, q, 0], twin
            ).wait_recv()

        @pl.when(core == 0)
        def _():
            rbuf[n, q, 0] = part[n, q, 0]

        return rbuf[n, q, 0].astype(F32) + rbuf[n, q, 1].astype(F32)

    def partial_close(n, q):
        remote(
            part.at[n, q, 1], rbuf.at[n, q, 1], ps.at[n, q, 1], pr.at[n, q, 1], twin
        ).wait_send()

        @pl.when(core == 1)
        def _():
            remote(
                part.at[n, q, 0], rbuf.at[n, q, 0], ps.at[n, q, 0], pr.at[n, q, 0], twin
            ).wait_send()

    for q in range(NQ):
        for c in range(2):
            term = jnp.dot(
                poly[...], panel[c, pl.ds(0, HALF), q * Q : (q + 1) * Q],
                preferred_element_type=F32,
            )
            yown[q, c] = term
            part[0, q, c] = term.astype(BF16)
        send_partial(0, q)
    rings = []
    for q in range(NQ):
        ypanel[q, core, pl.ds(0, B)] = reduced(0, q).astype(BF16)

        def yslot(c, at_row, rows, q=q):
            return ypanel.at[q, c, pl.ds(at_row, rows)]

        rings.append(gather(ypanel.at[q, core, pl.ds(0, B)], yslot, 1 + q))
        rings[q][0]()
    for q in range(NQ):
        rings[q][1]()
    for q in range(NQ):
        rings[q][2]()
        for c in range(2):
            term = jnp.dot(poly[...], ypanel[q, c], preferred_element_type=F32)
            part[1, q, c] = (2.0315 * term - 4.775 * yown[q, c]).astype(BF16)
        send_partial(1, q)
    scale = math.sqrt(N)
    for q in range(NQ):
        cols = slice(q * Q, (q + 1) * Q)
        total = 3.4445 * x_ref[:, cols].astype(F32) + reduced(1, q)
        out_ref[:, cols] = (total * scale).astype(BF16)

    close()
    other.wait_send()
    for c in ysend + zsend + gsend + hsend:
        c.wait_send()
    for q in range(NQ):
        rings[q][3]()
        for n in range(2):
            partial_close(n, q)


def on_device(iterate):
    dma = pltpu.SemaphoreType.DMA
    return pl.pallas_call(
        kernel,
        out_shape=jax.ShapeDtypeStruct((B, W), BF16),
        in_specs=[pl.BlockSpec(memory_space=pltpu.VMEM)],
        out_specs=pl.BlockSpec(memory_space=pltpu.VMEM),
        scratch_shapes=[
            pltpu.VMEM((2, HALF + B, W), BF16),
            pltpu.VMEM((NQ, 2, HALF, Q), BF16),
            pltpu.VMEM((B, HW), BF16),
            pltpu.VMEM((B, HW), F32),
            pltpu.VMEM((B, HW), BF16),
            pltpu.VMEM((B, HW), BF16),
            pltpu.VMEM((7, SH, HW), BF16),
            pltpu.VMEM((2, 8, SH, HW), BF16),
            pltpu.VMEM((B, HALF), BF16),
            pltpu.VMEM((2, NQ, 2, B, Q), BF16),
            pltpu.VMEM((2, NQ, 2, B, Q), BF16),
            pltpu.VMEM((NQ, 2, B, Q), F32),
            dma,
            dma((1 + NQ, 6)), dma((1 + NQ, 6)),
            dma((1 + NQ, 7)), dma((1 + NQ, 7)),
            dma((1,)), dma((2,)),
            dma((4,)), dma((4,)),
            dma((7,)), dma((7,)),
            dma((7,)), dma((7,)),
            dma((8,)), dma((8,)),
            dma((2, NQ, 2)), dma((2, NQ, 2)),
        ],
        compiler_params=pltpu.CompilerParams(
            collective_id=0, has_side_effects=True, vmem_limit_bytes=56 * 2**20
        ),
    )(iterate)


def solution(mesh):
    in_specs = (P("row", "col"),)
    out_specs = P("row", "col")
    return jax.shard_map(
        on_device, mesh=mesh, in_specs=in_specs, out_specs=out_specs, check_vma=False
    )
```

```python
import math

import jax
import jax.numpy as jnp
from jax import lax
from jax.experimental import pallas as pl
from jax.experimental.pallas import tpu as pltpu
from jax.sharding import PartitionSpec as P

N = 16384
B = 448
W = 512
S = 512
NX = 4
NJ = 3
NQ = 2
Q = W // NQ
HB = B // 2
PR = HB // 2
PC = S // 4
F32 = jnp.float32
BF16 = jnp.bfloat16
NT = (((1,), (1,)), ((), ()))
MESH = pl.DeviceIdType.MESH


def kernel(
    x_ref, out_ref, panel, ypanel, tsend, town, ybuf, zsrc, zbuf, gsh, agbuf, poly, mbuf,
    part, rbuf, yown, loc_sem, xs, xr, cs, cr, ls, lr, ys, yr, zs, zr, gs, gr, hs, hr,
    ms, mr, ps, pr,
):
    row = lax.axis_index("row")
    col = lax.axis_index("col")
    x = row % 4
    low = row // 4
    core = col % 2
    high = (col // 2) % 2
    z = col // 4

    def at(x_=None, low_=None, z_=None, high_=None, core_=None):
        x_ = x if x_ is None else x_
        low_ = low if low_ is None else low_
        z_ = z if z_ is None else z_
        high_ = high if high_ is None else high_
        core_ = core if core_ is None else core_
        return (low_ * 4 + x_, z_ * 4 + high_ * 2 + core_)

    def remote(src, dst, send, recv, dev):
        return pltpu.make_async_remote_copy(
            src_ref=src, dst_ref=dst, send_sem=send, recv_sem=recv,
            device_id=dev, device_id_type=MESH,
        )

    pend = []
    up = at(x_=(x + 1) % 4)
    down = at(x_=(x + 3) % 4)
    twin = at(core_=1 - core)
    across = at(high_=1 - high)
    other_low = low + core * (1 - 2 * low)
    mirror_to = at(x_=(x + 1) % 4, low_=other_low)
    mirror_from = at(x_=(x + 3) % 4, low_=other_low)

    barrier = pltpu.get_barrier_semaphore()
    peers = [up, down, twin, across, mirror_to, mirror_from]
    peers += [at(low_=1 - low, core_=k) for k in range(2)]
    peers += [at(z_=(z + d) % 8) for d in range(1, 8)]
    for dev in peers:
        pl.semaphore_signal(barrier, inc=1, device_id=dev, device_id_type=MESH)
    for c in range(2):
        for j in range(NJ):
            panel[c, j * S + B : (j + 1) * S, :] = jnp.zeros((S - B, W), BF16)
    panel[0, 3 * S + B : 4 * S, :] = jnp.zeros((S - B, W), BF16)
    panel[1, 3 * S + B : 4 * S, :] = jnp.zeros((S - B, W), BF16)
    for q in range(NQ):
        for c in range(2):
            for j in range(NX):
                ypanel[q, c, j * S + B : (j + 1) * S, :] = jnp.zeros((S - B, Q), BF16)
    pl.semaphore_wait(barrier, len(peers))

    h = B // 2

    def gather(own, slot, n):
        a, b = pl.ds(0, h), pl.ds(h, h)
        direct = [
            remote(own.at[a], slot(core, S, h), xs.at[n, 0], xr.at[n, 0], down),
            remote(own.at[b], slot(core, 3 * S + h, h), xs.at[n, 1], xr.at[n, 1], up),
            remote(own.at[b], slot(core, S + h, h), xs.at[n, 2], xr.at[n, 2], down),
            remote(own.at[a], slot(core, 3 * S, h), xs.at[n, 3], xr.at[n, 3], up),
        ]
        passed = [
            remote(slot(core, S, h), slot(core, 2 * S, h), xs.at[n, 4], xr.at[n, 4], down),
            remote(slot(core, 3 * S + h, h), slot(core, 2 * S + h, h), xs.at[n, 5], xr.at[n, 5], up),
        ]
        moves = direct + passed
        places = [S, 3 * S + h, S + h, 3 * S, 2 * S, 2 * S + h]
        cross = [
            remote(slot(core, p, h), slot(core, p, h), cs.at[n, k], cr.at[n, k], twin)
            for k, p in enumerate(places)
        ]
        cross.append(remote(own, slot(core, 0, B), cs.at[n, 6], cr.at[n, 6], twin))

        def start():
            cross[6].start()
            for k in range(3):
                direct[k].start()

        def relay(k):
            moves[k].wait_recv()
            if k < 2:
                passed[k].start()
            if k == 1:
                direct[3].start()
            cross[k].start()

        def done(ks):
            for k in ks:
                cross[k].wait_recv()

        def close():
            for c in moves + cross:
                c.wait_send()

        return start, relay, done, close

    def xslot(c, at_row, rows):
        return panel.at[c, pl.ds(at_row, rows)]

    start, relay, done, close = gather(x_ref, xslot, 0)
    start()
    other = remote(
        x_ref, panel.at[core, pl.ds(NX * S, B)], ls.at[0], lr.at[core], at(low_=1 - low, core_=1)
    )
    other.start()
    keep = pltpu.make_async_copy(x_ref, panel.at[core, pl.ds(0, B)], loc_sem)
    keep.start()
    keep.wait()
    done([6])

    left = core * NX * S

    def gram(half, j):
        rows = pl.ds(pl.multiple_of(left + half * HB, 32), HB)
        total = None
        for c in range(2):
            term = lax.dot_general(
                panel[c, rows, :], panel[c, pl.ds(j * S, S), :], NT, preferred_element_type=F32
            )
            total = term if total is None else total + term
        return total

    ysend = [remote(tsend.at[j], ybuf.at[j], ys.at[j], yr.at[j], across) for j in range(NJ)]

    def make(j):
        tsend[j] = gram(1 - high, j).astype(BF16)
        ysend[j].start()
        town[j] = gram(high, j)

    zsend = [
        [
            remote(
                zsrc.at[j, (z + d) % 8], zbuf.at[j, d - 1], zs.at[j, d - 1], zr.at[j, d - 1],
                at(z_=(z + d) % 8),
            )
            for d in (1, 7, 2, 6, 3, 5, 4)
        ]
        for j in range(NJ)
    ]

    def scatter(j):
        ysend[j].wait_recv()
        for p in range(8):
            rows = slice(p % 2 * PR, (p % 2 + 1) * PR)
            cols = slice(p // 2 * PC, (p // 2 + 1) * PC)
            zsrc[j, p] = (town[j, rows, cols] + ybuf[j, rows, cols].astype(F32)).astype(BF16)
        for c in zsend[j]:
            c.start()

    gsend = [
        [
            remote(
                gsh.at[j], agbuf.at[high, j, z], gs.at[j, d - 1], gr.at[j, d - 1],
                at(z_=(z + d) % 8),
            )
            for d in (1, 7, 2, 6, 3, 5, 4)
        ]
        for j in range(NJ)
    ]

    def spread(j):
        total = zsrc[j, z].astype(F32)
        for c in zsend[j]:
            c.wait_recv()
        for k in range(7):
            total = total + zbuf[j, k].astype(F32)
        gsh[j] = total.astype(BF16)
        for c in gsend[j]:
            c.start()
        agbuf[high, j, z] = total.astype(BF16)

    hsend = [
        remote(agbuf.at[high, j], agbuf.at[high, j], hs.at[j], hr.at[j], across)
        for j in range(NJ)
    ]

    def swap(j):
        for c in gsend[j]:
            c.wait_recv()
        hsend[j].start()

    mirror = remote(poly.at[:, pl.ds(S, S)], mbuf, ms.at[0], mr.at[0], mirror_to)

    def place(j):
        remote(
            agbuf.at[1 - high, j], agbuf.at[1 - high, j], hs.at[j], hr.at[j], across
        ).wait_recv()
        for half in range(2):
            for p in range(8):
                at_row = half * HB + p % 2 * PR
                at_col = j * S + p // 2 * PC
                poly[at_row : at_row + PR, at_col : at_col + PC] = agbuf[half, j, p]
        if j == 1:
            mirror.start()

    relay(0)
    relay(1)
    relay(2)

    @pl.when(core == 1)
    def _():
        for k in range(2):
            remote(
                x_ref, panel.at[k, pl.ds(NX * S, B)], ls.at[0], lr.at[k],
                at(low_=1 - low, core_=1),
            ).wait_recv()

    make(0)
    done([0, 2])
    make(1)
    scatter(0)
    relay(4)
    relay(5)
    done([4, 5])
    make(2)
    scatter(1)
    relay(3)
    spread(0)
    scatter(2)
    swap(0)
    spread(1)
    place(0)
    swap(1)
    spread(2)
    place(1)
    swap(2)
    done([1, 3])

    def send_partial(n, q):
        one = remote(
            part.at[n, q, 1], rbuf.at[n, q, core], ps.at[n, q, 1], pr.at[n, q, core],
            at(low_=other_low, core_=1),
        )
        one.start()

        @pl.when(core == 1)
        def _():
            remote(
                part.at[n, q, 0], rbuf.at[n, q, 1], ps.at[n, q, 0], pr.at[n, q, 1],
                at(low_=1 - low, core_=0),
            ).start()

    def reduced(n, q):
        remote(
            part.at[n, q, 1], rbuf.at[n, q, 1], ps.at[n, q, 1], pr.at[n, q, 1], twin
        ).wait_recv()

        @pl.when(core == 1)
        def _():
            remote(
                part.at[n, q, 0], rbuf.at[n, q, 0], ps.at[n, q, 0], pr.at[n, q, 0], twin
            ).wait_recv()

        @pl.when(core == 0)
        def _():
            rbuf[n, q, 0] = part[n, q, 0]

        return rbuf[n, q, 0].astype(F32) + rbuf[n, q, 1].astype(F32)

    def partial_close(n, q):
        remote(
            part.at[n, q, 1], rbuf.at[n, q, 1], ps.at[n, q, 1], pr.at[n, q, 1], twin
        ).wait_send()

        @pl.when(core == 1)
        def _():
            remote(
                part.at[n, q, 0], rbuf.at[n, q, 0], ps.at[n, q, 0], pr.at[n, q, 0], twin
            ).wait_send()

    def early(q, c):
        return jnp.dot(
            poly[:, 0 : 2 * S], panel[c, 0 : 2 * S, q * Q : (q + 1) * Q],
            preferred_element_type=F32,
        )

    for q in range(NQ):
        for c in range(2):
            yown[q, c] = early(q, c)
    place(2)
    mirror.wait_recv()
    turned = mbuf[...].astype(F32).T
    poly[:, 3 * S : 3 * S + B] = turned[0:B, :].astype(BF16)
    poly[:, 3 * S + B : 4 * S] = jnp.zeros((B, S - B), BF16)
    for q in range(NQ):
        for c in range(2):
            term = yown[q, c] + jnp.dot(
                poly[:, 2 * S : 4 * S], panel[c, 2 * S : 4 * S, q * Q : (q + 1) * Q],
                preferred_element_type=F32,
            )
            yown[q, c] = term
            part[0, q, c] = term.astype(BF16)
        send_partial(0, q)
    rings = []
    for q in range(NQ):
        ypanel[q, core, pl.ds(0, B)] = reduced(0, q).astype(BF16)

        def yslot(c, at_row, rows, q=q):
            return ypanel.at[q, c, pl.ds(at_row, rows)]

        rings.append(gather(ypanel.at[q, core, pl.ds(0, B)], yslot, 1 + q))
        rings[q][0]()
    for q in range(NQ):
        for k in range(6):
            rings[q][1](k)
    for q in range(NQ):
        rings[q][2](range(7))
        for c in range(2):
            term = jnp.dot(poly[...], ypanel[q, c], preferred_element_type=F32)
            part[1, q, c] = (2.0315 * term - 4.775 * yown[q, c]).astype(BF16)
        send_partial(1, q)
    scale = math.sqrt(N)
    for q in range(NQ):
        cols = slice(q * Q, (q + 1) * Q)
        total = 3.4445 * x_ref[:, cols].astype(F32) + reduced(1, q)
        out_ref[:, cols] = (total * scale).astype(BF16)

    close()
    other.wait_send()
    mirror.wait_send()
    for j in range(NJ):
        for c in [ysend[j], hsend[j]] + zsend[j] + gsend[j]:
            c.wait_send()
    for q in range(NQ):
        rings[q][3]()
        for n in range(2):
            partial_close(n, q)


def on_device(iterate):
    dma = pltpu.SemaphoreType.DMA
    return pl.pallas_call(
        kernel,
        out_shape=jax.ShapeDtypeStruct((B, W), BF16),
        in_specs=[pl.BlockSpec(memory_space=pltpu.VMEM)],
        out_specs=pl.BlockSpec(memory_space=pltpu.VMEM),
        scratch_shapes=[
            pltpu.VMEM((2, NX * S + B, W), BF16),
            pltpu.VMEM((NQ, 2, NX * S, Q), BF16),
            pltpu.VMEM((NJ, HB, S), BF16),
            pltpu.VMEM((NJ, HB, S), F32),
            pltpu.VMEM((NJ, HB, S), BF16),
            pltpu.VMEM((NJ, 8, PR, PC), BF16),
            pltpu.VMEM((NJ, 7, PR, PC), BF16),
            pltpu.VMEM((NJ, PR, PC), BF16),
            pltpu.VMEM((2, NJ, 8, PR, PC), BF16),
            pltpu.VMEM((B, NX * S), BF16),
            pltpu.VMEM((B, S), BF16),
            pltpu.VMEM((2, NQ, 2, B, Q), BF16),
            pltpu.VMEM((2, NQ, 2, B, Q), BF16),
            pltpu.VMEM((NQ, 2, B, Q), F32),
            dma,
            dma((1 + NQ, 6)), dma((1 + NQ, 6)),
            dma((1 + NQ, 7)), dma((1 + NQ, 7)),
            dma((1,)), dma((2,)),
            dma((NJ,)), dma((NJ,)),
            dma((NJ, 7)), dma((NJ, 7)),
            dma((NJ, 7)), dma((NJ, 7)),
            dma((NJ,)), dma((NJ,)),
            dma((1,)), dma((1,)),
            dma((2, NQ, 2)), dma((2, NQ, 2)),
        ],
        compiler_params=pltpu.CompilerParams(
            collective_id=0, has_side_effects=True, vmem_limit_bytes=56 * 2**20
        ),
    )(iterate)


def solution(mesh):
    in_specs = (P("row", "col"),)
    out_specs = P("row", "col")
    return jax.shard_map(
        on_device, mesh=mesh, in_specs=in_specs, out_specs=out_specs, check_vma=False
    )
```

```python
import math

import jax
import jax.numpy as jnp
from jax import lax
from jax.experimental import pallas as pl
from jax.experimental.pallas import tpu as pltpu
from jax.sharding import PartitionSpec as P

N = 16384
B = 448
W = 512
S = 512
NX = 4
NJ = 3
NQ = 4
Q = W // NQ
HB = B // 2
PR = HB // 2
PC = S // 4
F32 = jnp.float32
BF16 = jnp.bfloat16
NT = (((1,), (1,)), ((), ()))
MESH = pl.DeviceIdType.MESH


def kernel(
    x_ref, out_ref, panel, ypanel, tsend, town, ybuf, zsrc, zbuf, gsh, agbuf, poly, mfull,
    part, rbuf, yown, loc_sem, xs, xr, cs, cr, ls, lr, ys, yr, zs, zr, gs, gr, hs, hr,
    ms, mr, ps, pr,
):
    row = lax.axis_index("row")
    col = lax.axis_index("col")
    x = row % 4
    low = row // 4
    core = col % 2
    high = (col // 2) % 2
    z = col // 4

    def at(x_=None, low_=None, z_=None, high_=None, core_=None):
        x_ = x if x_ is None else x_
        low_ = low if low_ is None else low_
        z_ = z if z_ is None else z_
        high_ = high if high_ is None else high_
        core_ = core if core_ is None else core_
        return (low_ * 4 + x_, z_ * 4 + high_ * 2 + core_)

    def remote(src, dst, send, recv, dev):
        return pltpu.make_async_remote_copy(
            src_ref=src, dst_ref=dst, send_sem=send, recv_sem=recv,
            device_id=dev, device_id_type=MESH,
        )

    pend = []
    up = at(x_=(x + 1) % 4)
    down = at(x_=(x + 3) % 4)
    twin = at(core_=1 - core)
    across = at(high_=1 - high)
    other_low = low + core * (1 - 2 * low)
    mirror_to = at(x_=(x + 1) % 4, low_=other_low)
    mirror_from = at(x_=(x + 3) % 4, low_=other_low)

    barrier = pltpu.get_barrier_semaphore()
    peers = [up, down, twin, across, mirror_to, mirror_from]
    peers += [at(low_=1 - low, core_=k) for k in range(2)]
    peers += [at(z_=(z + d) % 8) for d in range(1, 8)]
    for dev in peers:
        pl.semaphore_signal(barrier, inc=1, device_id=dev, device_id_type=MESH)
    for c in range(2):
        for j in range(NJ):
            panel[c, j * S + B : (j + 1) * S, :] = jnp.zeros((S - B, W), BF16)
    panel[0, 3 * S + B : 4 * S, :] = jnp.zeros((S - B, W), BF16)
    panel[1, 3 * S + B : 4 * S, :] = jnp.zeros((S - B, W), BF16)
    for q in range(NQ):
        for c in range(2):
            for j in range(NX):
                ypanel[q, c, j * S + B : (j + 1) * S, :] = jnp.zeros((S - B, Q), BF16)
    pl.semaphore_wait(barrier, len(peers))

    h = B // 2

    def gather(own, slot, n):
        a, b = pl.ds(0, h), pl.ds(h, h)
        direct = [
            remote(own.at[a], slot(core, S, h), xs.at[n, 0], xr.at[n, 0], down),
            remote(own.at[b], slot(core, 3 * S + h, h), xs.at[n, 1], xr.at[n, 1], up),
            remote(own.at[b], slot(core, S + h, h), xs.at[n, 2], xr.at[n, 2], down),
            remote(own.at[a], slot(core, 3 * S, h), xs.at[n, 3], xr.at[n, 3], up),
        ]
        passed = [
            remote(slot(core, S, h), slot(core, 2 * S, h), xs.at[n, 4], xr.at[n, 4], down),
            remote(slot(core, 3 * S + h, h), slot(core, 2 * S + h, h), xs.at[n, 5], xr.at[n, 5], up),
        ]
        moves = direct + passed
        places = [S, 3 * S + h, S + h, 3 * S, 2 * S, 2 * S + h]
        cross = [
            remote(slot(core, p, h), slot(core, p, h), cs.at[n, k], cr.at[n, k], twin)
            for k, p in enumerate(places)
        ]
        cross.append(remote(own, slot(core, 0, B), cs.at[n, 6], cr.at[n, 6], twin))

        def start():
            cross[6].start()
            for c in direct:
                c.start()

        def relay(k):
            moves[k].wait_recv()
            if k < 2:
                passed[k].start()
            cross[k].start()

        def done(ks):
            for k in ks:
                cross[k].wait_recv()

        def close():
            for c in moves + cross:
                c.wait_send()

        return start, relay, done, close

    def xslot(c, at_row, rows):
        return panel.at[c, pl.ds(at_row, rows)]

    start, relay, done, close = gather(x_ref, xslot, 0)
    start()
    def other(k, c):
        half = (1 - high) if k == 0 else high
        rows = pl.multiple_of(half * HB, 32)
        return remote(
            x_ref.at[pl.ds(rows, HB)], panel.at[c, pl.ds(NX * S + rows, HB)], ls.at[k],
            lr.at[k, c], at(low_=1 - low, core_=1),
        )

    for k in range(2):
        other(k, core).start()
    keep = pltpu.make_async_copy(x_ref, panel.at[core, pl.ds(0, B)], loc_sem)
    keep.start()
    keep.wait()
    done([6])

    left = core * NX * S

    def gram(half, j):
        rows = pl.ds(pl.multiple_of(left + half * HB, 32), HB)
        total = None
        for c in range(2):
            term = lax.dot_general(
                panel[c, rows, :], panel[c, pl.ds(j * S, S), :], NT, preferred_element_type=F32
            )
            total = term if total is None else total + term
        return total

    ysend = [remote(tsend.at[j], ybuf.at[j], ys.at[j], yr.at[j], across) for j in range(NJ)]

    def make_sent(j):
        tsend[j] = gram(1 - high, j).astype(BF16)
        ysend[j].start()

    def make_kept(j):
        town[j] = gram(high, j)

    zsend = [
        [
            remote(
                zsrc.at[j, (z + d) % 8], zbuf.at[j, d - 1], zs.at[j, d - 1], zr.at[j, d - 1],
                at(z_=(z + d) % 8),
            )
            for d in (1, 7, 2, 6, 3, 5, 4)
        ]
        for j in range(NJ)
    ]

    def scatter(j):
        ysend[j].wait_recv()
        for p in range(8):
            rows = slice(p % 2 * PR, (p % 2 + 1) * PR)
            cols = slice(p // 2 * PC, (p // 2 + 1) * PC)
            zsrc[j, p] = (town[j, rows, cols] + ybuf[j, rows, cols].astype(F32)).astype(BF16)
        for c in zsend[j]:
            c.start()

    def over_z(src, j, origin, d, to):
        dst = agbuf.at[high, j, origin % 8]
        return remote(src, dst, gs.at[j, d - 1], gr.at[j, d - 1], at(z_=to % 8))

    gsend = [[over_z(gsh.at[j], j, z, d, z + d) for d in (1, 7, 2, 6)] for j in range(NX)]
    gpass = [
        [
            over_z(agbuf.at[high, j, o % 8], j, o, d, to)
            for o, d, to in ((z + 6, 3, z + 1), (z + 6, 4, z + 2), (z + 2, 5, z + 7))
        ]
        for j in range(NX)
    ]

    def arrived(j, d):
        over_z(gsh.at[j], j, z + 8 - d, d, z + 1).wait_recv()

    def spread(j):
        total = zsrc[j, z].astype(F32)
        for c in zsend[j]:
            c.wait_recv()
        for k in range(7):
            total = total + zbuf[j, k].astype(F32)
        gsh[j] = total.astype(BF16)
        for c in gsend[j]:
            c.start()
        if j == 1:
            mirror.start()
        agbuf[high, j, z] = total.astype(BF16)

    def forward(j):
        arrived(j, 2)
        gpass[j][0].start()
        gpass[j][1].start()
        arrived(j, 6)
        gpass[j][2].start()

    hsend = [
        remote(agbuf.at[high, j], agbuf.at[high, j], hs.at[j], hr.at[j], across)
        for j in range(NX)
    ]

    def swap(j):
        for d in (1, 7, 3, 5, 4):
            arrived(j, d)
        hsend[j].start()

    mirror = remote(gsh.at[1], gsh.at[3], ms.at[0], mr.at[0], mirror_to)

    def reflect():
        mirror.wait_recv()
        for c in gsend[3]:
            c.start()
        agbuf[high, 3, z] = gsh[3]

    def place(j):
        remote(
            agbuf.at[1 - high, j], agbuf.at[1 - high, j], hs.at[j], hr.at[j], across
        ).wait_recv()
        for half in range(2):
            for p in range(8):
                at_row = half * HB + p % 2 * PR
                at_col = p // 2 * PC
                if j == 3:
                    mfull[at_row : at_row + PR, at_col : at_col + PC] = agbuf[half, j, p].astype(F32)
                else:
                    at_col += j * S
                    poly[at_row : at_row + PR, at_col : at_col + PC] = agbuf[half, j, p]
        if j == 3:
            turned = mfull[...].T
            poly[:, 3 * S : 3 * S + B] = turned[0:B, :].astype(BF16)
            poly[:, 3 * S + B : 4 * S] = jnp.zeros((B, S - B), BF16)

    def wait_other(k):
        for c in range(2):
            other(k, c).wait_recv()

    @pl.when(core == 0)
    def _():
        make_sent(0)
        make_kept(0)
        relay(0)
        relay(1)
        scatter(0)
        relay(2)
        done([0, 2])
        make_sent(1)
        make_kept(1)
        relay(3)
        relay(5)
        relay(4)
        done([4, 5])
        make_sent(2)
        make_kept(2)
        spread(0)
        scatter(1)
        forward(0)
        swap(0)
        scatter(2)
        spread(1)
        place(0)
        forward(1)
        reflect()
        spread(2)
        swap(1)
        forward(3)
        forward(2)
        place(1)
        swap(3)
        swap(2)

    @pl.when(core == 1)
    def _():
        relay(0)
        relay(1)
        wait_other(0)
        make_sent(0)
        relay(2)
        done([0, 2])
        make_sent(1)
        relay(3)
        wait_other(1)
        make_kept(0)
        scatter(0)
        relay(5)
        make_kept(1)
        relay(4)
        done([4, 5])
        make_sent(2)
        make_kept(2)
        scatter(1)
        spread(0)
        forward(0)
        scatter(2)
        spread(1)
        swap(0)
        forward(1)
        reflect()
        spread(2)
        swap(1)
        forward(3)
        forward(2)
        place(0)
        place(1)
        swap(3)
        swap(2)

    done([1, 3])

    def send_partial(n, q):
        one = remote(
            part.at[n, q, 1], rbuf.at[n, q, core], ps.at[n, q, 1], pr.at[n, q, core],
            at(low_=other_low, core_=1),
        )
        one.start()

        @pl.when(core == 1)
        def _():
            remote(
                part.at[n, q, 0], rbuf.at[n, q, 1], ps.at[n, q, 0], pr.at[n, q, 1],
                at(low_=1 - low, core_=0),
            ).start()

    def reduced(n, q):
        remote(
            part.at[n, q, 1], rbuf.at[n, q, 1], ps.at[n, q, 1], pr.at[n, q, 1], twin
        ).wait_recv()

        @pl.when(core == 1)
        def _():
            remote(
                part.at[n, q, 0], rbuf.at[n, q, 0], ps.at[n, q, 0], pr.at[n, q, 0], twin
            ).wait_recv()

        @pl.when(core == 0)
        def _():
            rbuf[n, q, 0] = part[n, q, 0]

        return rbuf[n, q, 0].astype(F32) + rbuf[n, q, 1].astype(F32)

    def partial_close(n, q):
        remote(
            part.at[n, q, 1], rbuf.at[n, q, 1], ps.at[n, q, 1], pr.at[n, q, 1], twin
        ).wait_send()

        @pl.when(core == 1)
        def _():
            remote(
                part.at[n, q, 0], rbuf.at[n, q, 0], ps.at[n, q, 0], pr.at[n, q, 0], twin
            ).wait_send()

    def both(q, rows):
        cols = slice(q * Q, (q + 1) * Q)
        return jnp.concatenate([panel[0, rows, cols], panel[1, rows, cols]], axis=1)

    for q in range(NQ):
        yown[q] = jnp.dot(
            poly[:, 0 : 2 * S], both(q, slice(0, 2 * S)), preferred_element_type=F32
        )
    place(3)
    place(2)
    for q in range(NQ):
        term = yown[q] + jnp.dot(
            poly[:, 2 * S : 4 * S], both(q, slice(2 * S, 4 * S)), preferred_element_type=F32
        )
        yown[q] = term
        for c in range(2):
            part[0, q, c] = term[:, c * Q : (c + 1) * Q].astype(BF16)
        send_partial(0, q)
    rings = []

    def begin(q):
        ypanel[q, core, pl.ds(0, B)] = reduced(0, q).astype(BF16)

        def yslot(c, at_row, rows):
            return ypanel.at[q, c, pl.ds(at_row, rows)]

        rings.append(gather(ypanel.at[q, core, pl.ds(0, B)], yslot, 1 + q))
        rings[q][0]()

    def finish(q):
        rings[q][2](range(7))
        both_y = jnp.concatenate([ypanel[q, 0], ypanel[q, 1]], axis=1)
        term = jnp.dot(poly[...], both_y, preferred_element_type=F32)
        term = 2.0315 * term - 4.775 * yown[q]
        for c in range(2):
            part[1, q, c] = term[:, c * Q : (c + 1) * Q].astype(BF16)
        send_partial(1, q)

    for t in range(NQ + 3):
        if t < NQ:
            begin(t)
        for back, ks in ((1, (0, 1)), (2, (2, 3)), (3, (4, 5))):
            if 0 <= t - back < NQ:
                for k in ks:
                    rings[t - back][1](k)
        if t >= 3:
            finish(t - 3)
    scale = math.sqrt(N)
    for q in range(NQ):
        cols = slice(q * Q, (q + 1) * Q)
        total = 3.4445 * x_ref[:, cols].astype(F32) + reduced(1, q)
        out_ref[:, cols] = (total * scale).astype(BF16)

    close()
    for k in range(2):
        other(k, core).wait_send()
    mirror.wait_send()
    for j in range(NJ):
        for c in [ysend[j]] + zsend[j]:
            c.wait_send()
    for j in range(NX):
        for c in [hsend[j]] + gsend[j] + gpass[j]:
            c.wait_send()
    for q in range(NQ):
        rings[q][3]()
        for n in range(2):
            partial_close(n, q)


def on_device(iterate):
    dma = pltpu.SemaphoreType.DMA
    return pl.pallas_call(
        kernel,
        out_shape=jax.ShapeDtypeStruct((B, W), BF16),
        in_specs=[pl.BlockSpec(memory_space=pltpu.VMEM)],
        out_specs=pl.BlockSpec(memory_space=pltpu.VMEM),
        scratch_shapes=[
            pltpu.VMEM((2, NX * S + B, W), BF16),
            pltpu.VMEM((NQ, 2, NX * S, Q), BF16),
            pltpu.VMEM((NJ, HB, S), BF16),
            pltpu.VMEM((NJ, HB, S), F32),
            pltpu.VMEM((NJ, HB, S), BF16),
            pltpu.VMEM((NJ, 8, PR, PC), BF16),
            pltpu.VMEM((NJ, 7, PR, PC), BF16),
            pltpu.VMEM((NX, PR, PC), BF16),
            pltpu.VMEM((2, NX, 8, PR, PC), BF16),
            pltpu.VMEM((B, NX * S), BF16),
            pltpu.VMEM((B, S), F32),
            pltpu.VMEM((2, NQ, 2, B, Q), BF16),
            pltpu.VMEM((2, NQ, 2, B, Q), BF16),
            pltpu.VMEM((NQ, B, 2 * Q), F32),
            dma,
            dma((1 + NQ, 6)), dma((1 + NQ, 6)),
            dma((1 + NQ, 7)), dma((1 + NQ, 7)),
            dma((2,)), dma((2, 2)),
            dma((NJ,)), dma((NJ,)),
            dma((NJ, 7)), dma((NJ, 7)),
            dma((NX, 7)), dma((NX, 7)),
            dma((NX,)), dma((NX,)),
            dma((1,)), dma((1,)),
            dma((2, NQ, 2)), dma((2, NQ, 2)),
        ],
        compiler_params=pltpu.CompilerParams(
            collective_id=0, has_side_effects=True, vmem_limit_bytes=56 * 2**20
        ),
    )(iterate)


def solution(mesh):
    in_specs = (P("row", "col"),)
    out_specs = P("row", "col")
    return jax.shard_map(
        on_device, mesh=mesh, in_specs=in_specs, out_specs=out_specs, check_vma=False
    )
```

```python
import math

import jax
import jax.numpy as jnp
from jax import lax
from jax.experimental import pallas as pl
from jax.experimental.pallas import tpu as pltpu
from jax.sharding import PartitionSpec as P

N = 16384
B = 448
W = 512
S = 512
NX = 4
NJ = 3
NQ = 4
Q = W // NQ
HB = B // 2
PR = HB // 2
PC = S // 4
F32 = jnp.float32
BF16 = jnp.bfloat16
NT = (((1,), (1,)), ((), ()))
MESH = pl.DeviceIdType.MESH


def kernel(
    x_ref, out_ref, panel, ypanel, tsend, town, ybuf, zsrc, zbuf, gsh, agbuf, poly, mfull,
    part, rbuf, yown, loc_sem, xs, xr, cs, cr, ls, lr, ys, yr, zs, zr, gs, gr, hs, hr,
    ms, mr, ps, pr,
):
    row = lax.axis_index("row")
    col = lax.axis_index("col")
    x = row % 4
    low = row // 4
    core = col % 2
    high = (col // 2) % 2
    z = col // 4

    def at(x_=None, low_=None, z_=None, high_=None, core_=None):
        x_ = x if x_ is None else x_
        low_ = low if low_ is None else low_
        z_ = z if z_ is None else z_
        high_ = high if high_ is None else high_
        core_ = core if core_ is None else core_
        return (low_ * 4 + x_, z_ * 4 + high_ * 2 + core_)

    def remote(src, dst, send, recv, dev):
        return pltpu.make_async_remote_copy(
            src_ref=src, dst_ref=dst, send_sem=send, recv_sem=recv,
            device_id=dev, device_id_type=MESH,
        )

    pend = []
    up = at(x_=(x + 1) % 4)
    down = at(x_=(x + 3) % 4)
    twin = at(core_=1 - core)
    across = at(high_=1 - high)
    other_low = low + core * (1 - 2 * low)
    mirror_to = at(x_=(x + 1) % 4, low_=other_low)
    mirror_from = at(x_=(x + 3) % 4, low_=other_low)

    barrier = pltpu.get_barrier_semaphore()
    peers = [up, down, twin, across, mirror_to, mirror_from]
    peers += [at(low_=1 - low, core_=k) for k in range(2)]
    peers += [at(z_=(z + d) % 8) for d in range(1, 8)]
    for dev in peers:
        pl.semaphore_signal(barrier, inc=1, device_id=dev, device_id_type=MESH)
    for c in range(2):
        for j in range(NJ):
            panel[c, j * S + B : (j + 1) * S, :] = jnp.zeros((S - B, W), BF16)
    panel[0, 3 * S + B : 4 * S, :] = jnp.zeros((S - B, W), BF16)
    panel[1, 3 * S + B : 4 * S, :] = jnp.zeros((S - B, W), BF16)
    for q in range(NQ):
        for c in range(2):
            for j in range(NX):
                ypanel[q, c, j * S + B : (j + 1) * S, :] = jnp.zeros((S - B, Q), BF16)
    pl.semaphore_wait(barrier, len(peers))

    h = B // 2

    def gather(own, slot, n):
        a, b = pl.ds(0, h), pl.ds(h, h)
        direct = [
            remote(own.at[a], slot(core, S, h), xs.at[n, 0], xr.at[n, 0], down),
            remote(own.at[b], slot(core, 3 * S + h, h), xs.at[n, 1], xr.at[n, 1], up),
            remote(own.at[b], slot(core, S + h, h), xs.at[n, 2], xr.at[n, 2], down),
            remote(own.at[a], slot(core, 3 * S, h), xs.at[n, 3], xr.at[n, 3], up),
        ]
        passed = [
            remote(slot(core, S, h), slot(core, 2 * S, h), xs.at[n, 4], xr.at[n, 4], down),
            remote(slot(core, 3 * S + h, h), slot(core, 2 * S + h, h), xs.at[n, 5], xr.at[n, 5], up),
        ]
        moves = direct + passed
        places = [S, 3 * S + h, S + h, 3 * S, 2 * S, 2 * S + h]
        cross = [
            remote(slot(core, p, h), slot(core, p, h), cs.at[n, k], cr.at[n, k], twin)
            for k, p in enumerate(places)
        ]
        cross.append(remote(own, slot(core, 0, B), cs.at[n, 6], cr.at[n, 6], twin))

        def start():
            cross[6].start()
            for c in direct:
                c.start()

        def relay(k):
            moves[k].wait_recv()
            if k < 2:
                passed[k].start()
            cross[k].start()

        def done(ks):
            for k in ks:
                cross[k].wait_recv()

        def close():
            for c in moves + cross:
                c.wait_send()

        return start, relay, done, close

    def xslot(c, at_row, rows):
        return panel.at[c, pl.ds(at_row, rows)]

    start, relay, done, close = gather(x_ref, xslot, 0)
    start()
    def other(k, c):
        half = (1 - high) if k == 0 else high
        rows = pl.multiple_of(half * HB, 32)
        return remote(
            x_ref.at[pl.ds(rows, HB)], panel.at[c, pl.ds(NX * S + rows, HB)], ls.at[k],
            lr.at[k, c], at(low_=1 - low, core_=1),
        )

    for k in range(2):
        other(k, core).start()
    keep = pltpu.make_async_copy(x_ref, panel.at[core, pl.ds(0, B)], loc_sem)
    keep.start()
    keep.wait()
    done([6])

    left = core * NX * S

    def gram(half, j):
        rows = pl.ds(pl.multiple_of(left + half * HB, 32), HB)
        total = None
        for c in range(2):
            term = lax.dot_general(
                panel[c, rows, :], panel[c, pl.ds(j * S, S), :], NT, preferred_element_type=F32
            )
            total = term if total is None else total + term
        return total

    ysend = [remote(tsend.at[j], ybuf.at[j], ys.at[j], yr.at[j], across) for j in range(NJ)]

    def make_sent(j):
        tsend[j] = gram(1 - high, j).astype(BF16)
        ysend[j].start()

    def make_kept(j):
        town[j] = gram(high, j)

    zsend = [
        [
            remote(
                zsrc.at[j, (z + d) % 8], zbuf.at[j, d - 1], zs.at[j, d - 1], zr.at[j, d - 1],
                at(z_=(z + d) % 8),
            )
            for d in (1, 7, 2, 6, 3, 5, 4)
        ]
        for j in range(NJ)
    ]

    def scatter(j):
        ysend[j].wait_recv()
        for p in range(8):
            rows = slice(p % 2 * PR, (p % 2 + 1) * PR)
            cols = slice(p // 2 * PC, (p // 2 + 1) * PC)
            zsrc[j, p] = (town[j, rows, cols] + ybuf[j, rows, cols].astype(F32)).astype(BF16)
        for c in zsend[j]:
            c.start()

    def over_z(src, j, origin, d, to):
        dst = agbuf.at[high, j, origin % 8]
        return remote(src, dst, gs.at[j, d - 1], gr.at[j, d - 1], at(z_=to % 8))

    gsend = [
        [over_z(gsh.at[j], j, z, d, z + d) for d in (1, 7, 2, 6, 3, 5, 4)] for j in range(NX)
    ]

    def arrived(j, d):
        over_z(gsh.at[j], j, z + 8 - d, d, z + 1).wait_recv()

    def spread(j):
        total = zsrc[j, z].astype(F32)
        for c in zsend[j]:
            c.wait_recv()
        for k in range(7):
            total = total + zbuf[j, k].astype(F32)
        gsh[j] = total.astype(BF16)
        for c in gsend[j]:
            c.start()
        if j == 1:
            mirror.start()
        agbuf[high, j, z] = total.astype(BF16)

    hsend = [
        remote(agbuf.at[high, j], agbuf.at[high, j], hs.at[j], hr.at[j], across)
        for j in range(NX)
    ]

    def swap(j):
        for d in range(1, 8):
            arrived(j, d)
        hsend[j].start()

    mirror = remote(gsh.at[1], gsh.at[3], ms.at[0], mr.at[0], mirror_to)

    def reflect():
        mirror.wait_recv()
        for c in gsend[3]:
            c.start()
        agbuf[high, 3, z] = gsh[3]

    def place(j):
        remote(
            agbuf.at[1 - high, j], agbuf.at[1 - high, j], hs.at[j], hr.at[j], across
        ).wait_recv()
        for half in range(2):
            for p in range(8):
                at_row = half * HB + p % 2 * PR
                at_col = p // 2 * PC
                if j == 3:
                    mfull[at_row : at_row + PR, at_col : at_col + PC] = agbuf[half, j, p].astype(F32)
                else:
                    at_col += j * S
                    poly[at_row : at_row + PR, at_col : at_col + PC] = agbuf[half, j, p]
        if j == 3:
            turned = mfull[...].T
            poly[:, 3 * S : 3 * S + B] = turned[0:B, :].astype(BF16)
            poly[:, 3 * S + B : 4 * S] = jnp.zeros((B, S - B), BF16)

    def wait_other(k):
        for c in range(2):
            other(k, c).wait_recv()

    @pl.when(core == 0)
    def _():
        make_sent(0)
        make_kept(0)
        relay(0)
        relay(1)
        scatter(0)
        relay(2)
        done([0, 2])
        make_sent(1)
        make_kept(1)
        relay(3)
        relay(5)
        relay(4)
        done([4, 5])
        make_sent(2)
        make_kept(2)
        spread(0)
        scatter(1)
        swap(0)
        scatter(2)
        spread(1)
        reflect()
        spread(2)
        swap(1)
        swap(3)
        place(0)
        swap(2)
        place(1)

    @pl.when(core == 1)
    def _():
        relay(0)
        relay(1)
        wait_other(0)
        make_sent(0)
        relay(2)
        done([0, 2])
        make_sent(1)
        relay(3)
        wait_other(1)
        make_kept(0)
        scatter(0)
        relay(5)
        make_kept(1)
        relay(4)
        done([4, 5])
        make_sent(2)
        make_kept(2)
        scatter(1)
        spread(0)
        scatter(2)
        spread(1)
        reflect()
        swap(0)
        spread(2)
        swap(1)
        swap(3)
        place(0)
        swap(2)
        place(1)

    done([1, 3])

    def send_partial(n, q):
        one = remote(
            part.at[n, q, 1], rbuf.at[n, q, core], ps.at[n, q, 1], pr.at[n, q, core],
            at(low_=other_low, core_=1),
        )
        one.start()

        @pl.when(core == 1)
        def _():
            remote(
                part.at[n, q, 0], rbuf.at[n, q, 1], ps.at[n, q, 0], pr.at[n, q, 1],
                at(low_=1 - low, core_=0),
            ).start()

    def reduced(n, q):
        remote(
            part.at[n, q, 1], rbuf.at[n, q, 1], ps.at[n, q, 1], pr.at[n, q, 1], twin
        ).wait_recv()

        @pl.when(core == 1)
        def _():
            remote(
                part.at[n, q, 0], rbuf.at[n, q, 0], ps.at[n, q, 0], pr.at[n, q, 0], twin
            ).wait_recv()

        @pl.when(core == 0)
        def _():
            rbuf[n, q, 0] = part[n, q, 0]

        return rbuf[n, q, 0].astype(F32) + rbuf[n, q, 1].astype(F32)

    def partial_close(n, q):
        remote(
            part.at[n, q, 1], rbuf.at[n, q, 1], ps.at[n, q, 1], pr.at[n, q, 1], twin
        ).wait_send()

        @pl.when(core == 1)
        def _():
            remote(
                part.at[n, q, 0], rbuf.at[n, q, 0], ps.at[n, q, 0], pr.at[n, q, 0], twin
            ).wait_send()

    def both(q, rows):
        cols = slice(q * Q, (q + 1) * Q)
        return jnp.concatenate([panel[0, rows, cols], panel[1, rows, cols]], axis=1)

    for q in range(NQ):
        yown[q] = jnp.dot(
            poly[:, 0 : 2 * S], both(q, slice(0, 2 * S)), preferred_element_type=F32
        )
    place(3)
    place(2)
    for q in range(NQ):
        term = yown[q] + jnp.dot(
            poly[:, 2 * S : 4 * S], both(q, slice(2 * S, 4 * S)), preferred_element_type=F32
        )
        yown[q] = term
        for c in range(2):
            part[0, q, c] = term[:, c * Q : (c + 1) * Q].astype(BF16)
        send_partial(0, q)
    rings = []

    def begin(q):
        ypanel[q, core, pl.ds(0, B)] = reduced(0, q).astype(BF16)

        def yslot(c, at_row, rows):
            return ypanel.at[q, c, pl.ds(at_row, rows)]

        rings.append(gather(ypanel.at[q, core, pl.ds(0, B)], yslot, 1 + q))
        rings[q][0]()

    def finish(q):
        rings[q][2](range(7))
        both_y = jnp.concatenate([ypanel[q, 0], ypanel[q, 1]], axis=1)
        term = jnp.dot(poly[...], both_y, preferred_element_type=F32)
        term = 2.0315 * term - 4.775 * yown[q]
        for c in range(2):
            part[1, q, c] = term[:, c * Q : (c + 1) * Q].astype(BF16)
        send_partial(1, q)

    for t in range(NQ + 3):
        if t < NQ:
            begin(t)
        for back, ks in ((1, (0, 1)), (2, (2, 3)), (3, (4, 5))):
            if 0 <= t - back < NQ:
                for k in ks:
                    rings[t - back][1](k)
        if t >= 3:
            finish(t - 3)
    scale = math.sqrt(N)
    for q in range(NQ):
        cols = slice(q * Q, (q + 1) * Q)
        total = 3.4445 * x_ref[:, cols].astype(F32) + reduced(1, q)
        out_ref[:, cols] = (total * scale).astype(BF16)

    close()
    for k in range(2):
        other(k, core).wait_send()
    mirror.wait_send()
    for j in range(NJ):
        for c in [ysend[j]] + zsend[j]:
            c.wait_send()
    for j in range(NX):
        for c in [hsend[j]] + gsend[j]:
            c.wait_send()
    for q in range(NQ):
        rings[q][3]()
        for n in range(2):
            partial_close(n, q)


def on_device(iterate):
    dma = pltpu.SemaphoreType.DMA
    return pl.pallas_call(
        kernel,
        out_shape=jax.ShapeDtypeStruct((B, W), BF16),
        in_specs=[pl.BlockSpec(memory_space=pltpu.VMEM)],
        out_specs=pl.BlockSpec(memory_space=pltpu.VMEM),
        scratch_shapes=[
            pltpu.VMEM((2, NX * S + B, W), BF16),
            pltpu.VMEM((NQ, 2, NX * S, Q), BF16),
            pltpu.VMEM((NJ, HB, S), BF16),
            pltpu.VMEM((NJ, HB, S), F32),
            pltpu.VMEM((NJ, HB, S), BF16),
            pltpu.VMEM((NJ, 8, PR, PC), BF16),
            pltpu.VMEM((NJ, 7, PR, PC), BF16),
            pltpu.VMEM((NX, PR, PC), BF16),
            pltpu.VMEM((2, NX, 8, PR, PC), BF16),
            pltpu.VMEM((B, NX * S), BF16),
            pltpu.VMEM((B, S), F32),
            pltpu.VMEM((2, NQ, 2, B, Q), BF16),
            pltpu.VMEM((2, NQ, 2, B, Q), BF16),
            pltpu.VMEM((NQ, B, 2 * Q), F32),
            dma,
            dma((1 + NQ, 6)), dma((1 + NQ, 6)),
            dma((1 + NQ, 7)), dma((1 + NQ, 7)),
            dma((2,)), dma((2, 2)),
            dma((NJ,)), dma((NJ,)),
            dma((NJ, 7)), dma((NJ, 7)),
            dma((NX, 7)), dma((NX, 7)),
            dma((NX,)), dma((NX,)),
            dma((1,)), dma((1,)),
            dma((2, NQ, 2)), dma((2, NQ, 2)),
        ],
        compiler_params=pltpu.CompilerParams(
            collective_id=0, has_side_effects=True, vmem_limit_bytes=56 * 2**20
        ),
    )(iterate)


def solution(mesh):
    in_specs = (P("row", "col"),)
    out_specs = P("row", "col")
    return jax.shard_map(
        on_device, mesh=mesh, in_specs=in_specs, out_specs=out_specs, check_vma=False
    )
```

```python
import math

import jax
import jax.numpy as jnp
from jax import lax
from jax.experimental import pallas as pl
from jax.experimental.pallas import tpu as pltpu
from jax.sharding import PartitionSpec as P

N = 16384
B = 448
W = 512
S = 512
NX = 4
NJ = 3
NQ = 4
Q = W // NQ
HB = B // 2
PR = HB // 2
PC = S // 4
F32 = jnp.float32
BF16 = jnp.bfloat16
NT = (((1,), (1,)), ((), ()))
MESH = pl.DeviceIdType.MESH


def kernel(
    x_ref, out_ref, panel, ypanel, tsend, town, ybuf, zsrc, zbuf, gsh, agbuf, poly, mfull,
    part, rbuf, yown, loc_sem, xs, xr, cs, cr, ls, lr, ys, yr, zs, zr, gs, gr, hs, hr,
    ms, mr, ps, pr,
):
    row = lax.axis_index("row")
    col = lax.axis_index("col")
    x = row % 4
    low = row // 4
    core = col % 2
    high = (col // 2) % 2
    z = col // 4

    def at(x_=None, low_=None, z_=None, high_=None, core_=None):
        x_ = x if x_ is None else x_
        low_ = low if low_ is None else low_
        z_ = z if z_ is None else z_
        high_ = high if high_ is None else high_
        core_ = core if core_ is None else core_
        return (low_ * 4 + x_, z_ * 4 + high_ * 2 + core_)

    def remote(src, dst, send, recv, dev):
        return pltpu.make_async_remote_copy(
            src_ref=src, dst_ref=dst, send_sem=send, recv_sem=recv,
            device_id=dev, device_id_type=MESH,
        )

    pend = []
    up = at(x_=(x + 1) % 4)
    down = at(x_=(x + 3) % 4)
    twin = at(core_=1 - core)
    across = at(high_=1 - high)
    other_low = low + core * (1 - 2 * low)
    mirror_to = at(x_=(x + 1) % 4, low_=other_low)
    mirror_from = at(x_=(x + 3) % 4, low_=other_low)

    barrier = pltpu.get_barrier_semaphore()
    peers = [up, down, twin, across, mirror_to, mirror_from]
    peers += [at(low_=1 - low, core_=k) for k in range(2)]
    peers += [at(z_=(z + d) % 8) for d in range(1, 8)]
    for dev in peers:
        pl.semaphore_signal(barrier, inc=1, device_id=dev, device_id_type=MESH)
    for c in range(2):
        for j in range(NJ):
            panel[c, j * S + B : (j + 1) * S, :] = jnp.zeros((S - B, W), BF16)
    panel[0, 3 * S + B : 4 * S, :] = jnp.zeros((S - B, W), BF16)
    panel[1, 3 * S + B : 4 * S, :] = jnp.zeros((S - B, W), BF16)
    for q in range(NQ):
        for c in range(2):
            for j in range(NX):
                ypanel[q, c, j * S + B : (j + 1) * S, :] = jnp.zeros((S - B, Q), BF16)
    pl.semaphore_wait(barrier, len(peers))

    h = B // 2

    def gather(own, slot, n):
        a, b = pl.ds(0, h), pl.ds(h, h)
        direct = [
            remote(own.at[a], slot(core, S, h), xs.at[n, 0], xr.at[n, 0], down),
            remote(own.at[b], slot(core, 3 * S + h, h), xs.at[n, 1], xr.at[n, 1], up),
            remote(own.at[b], slot(core, S + h, h), xs.at[n, 2], xr.at[n, 2], down),
            remote(own.at[a], slot(core, 3 * S, h), xs.at[n, 3], xr.at[n, 3], up),
        ]
        passed = [
            remote(slot(core, S, h), slot(core, 2 * S, h), xs.at[n, 4], xr.at[n, 4], down),
            remote(slot(core, 3 * S + h, h), slot(core, 2 * S + h, h), xs.at[n, 5], xr.at[n, 5], up),
        ]
        moves = direct + passed
        places = [S, 3 * S + h, S + h, 3 * S, 2 * S, 2 * S + h]
        cross = [
            remote(slot(core, p, h), slot(core, p, h), cs.at[n, k], cr.at[n, k], twin)
            for k, p in enumerate(places)
        ]
        cross.append(remote(own, slot(core, 0, B), cs.at[n, 6], cr.at[n, 6], twin))

        def start():
            cross[6].start()
            for c in direct:
                c.start()

        def relay(k):
            moves[k].wait_recv()
            if k < 2:
                passed[k].start()
            cross[k].start()

        def done(ks):
            for k in ks:
                cross[k].wait_recv()

        def close():
            for c in moves + cross:
                c.wait_send()

        return start, relay, done, close

    def xslot(c, at_row, rows):
        return panel.at[c, pl.ds(at_row, rows)]

    start, relay, done, close = gather(x_ref, xslot, 0)
    start()
    def other(k, c):
        half = (1 - high) if k == 0 else high
        rows = pl.multiple_of(half * HB, 32)
        return remote(
            x_ref.at[pl.ds(rows, HB)], panel.at[c, pl.ds(NX * S + rows, HB)], ls.at[k],
            lr.at[k, c], at(low_=1 - low, core_=1),
        )

    for k in range(2):
        other(k, core).start()
    keep = pltpu.make_async_copy(x_ref, panel.at[core, pl.ds(0, B)], loc_sem)
    keep.start()
    keep.wait()
    done([6])

    left = core * NX * S

    def gram(half, j):
        rows = pl.ds(pl.multiple_of(left + half * HB, 32), HB)
        total = None
        for c in range(2):
            term = lax.dot_general(
                panel[c, rows, :], panel[c, pl.ds(j * S, S), :], NT, preferred_element_type=F32
            )
            total = term if total is None else total + term
        return total

    ysend = [remote(tsend.at[j], ybuf.at[j], ys.at[j], yr.at[j], across) for j in range(NJ)]

    def make_sent(j):
        tsend[j] = gram(1 - high, j).astype(BF16)
        ysend[j].start()

    def make_kept(j):
        town[j] = gram(high, j)

    zsend = [
        [
            remote(
                zsrc.at[j, (z + d) % 8], zbuf.at[j, d - 1], zs.at[j, d - 1], zr.at[j, d - 1],
                at(z_=(z + d) % 8),
            )
            for d in (1, 7, 2, 6, 3, 5, 4)
        ]
        for j in range(NJ)
    ]

    def scatter(j):
        ysend[j].wait_recv()
        for p in range(8):
            rows = slice(p % 2 * PR, (p % 2 + 1) * PR)
            cols = slice(p // 2 * PC, (p // 2 + 1) * PC)
            zsrc[j, p] = (town[j, rows, cols] + ybuf[j, rows, cols].astype(F32)).astype(BF16)
        for c in zsend[j]:
            c.start()

    def over_z(src, j, origin, d, to):
        dst = agbuf.at[high, j, origin % 8]
        return remote(src, dst, gs.at[j, d - 1], gr.at[j, d - 1], at(z_=to % 8))

    gsend = [
        [over_z(gsh.at[j], j, z, d, z + d) for d in (1, 7, 2, 6, 3, 5, 4)] for j in range(NX)
    ]

    def arrived(j, d):
        over_z(gsh.at[j], j, z + 8 - d, d, z + 1).wait_recv()

    def spread(j):
        total = zsrc[j, z].astype(F32)
        for c in zsend[j]:
            c.wait_recv()
        for k in range(7):
            total = total + zbuf[j, k].astype(F32)
        gsh[j] = total.astype(BF16)
        for c in gsend[j]:
            c.start()
        if j == 1:
            mirror.start()
        agbuf[high, j, z] = total.astype(BF16)
        hsend[j][0].start()

    hsend = [
        [
            remote(
                agbuf.at[high, j, (z + 8 - d) % 8], agbuf.at[high, j, (z + 8 - d) % 8],
                hs.at[j, d], hr.at[j, d], across,
            )
            for d in range(8)
        ]
        for j in range(NX)
    ]

    def swap(j):
        for d in (1, 7, 2, 6, 3, 5, 4):
            arrived(j, d)
            hsend[j][d].start()

    mirror = remote(gsh.at[1], gsh.at[3], ms.at[0], mr.at[0], mirror_to)

    def reflect():
        mirror.wait_recv()
        for c in gsend[3]:
            c.start()
        agbuf[high, 3, z] = gsh[3]
        hsend[3][0].start()

    def place(j):
        for c in hsend[j]:
            c.wait_recv()
        for half in range(2):
            for p in range(8):
                at_row = half * HB + p % 2 * PR
                at_col = p // 2 * PC
                if j == 3:
                    mfull[at_row : at_row + PR, at_col : at_col + PC] = agbuf[half, j, p].astype(F32)
                else:
                    at_col += j * S
                    poly[at_row : at_row + PR, at_col : at_col + PC] = agbuf[half, j, p]
        if j == 3:
            turned = mfull[...].T
            poly[:, 3 * S : 3 * S + B] = turned[0:B, :].astype(BF16)
            poly[:, 3 * S + B : 4 * S] = jnp.zeros((B, S - B), BF16)

    def wait_other(k):
        for c in range(2):
            other(k, c).wait_recv()

    @pl.when(core == 0)
    def _():
        make_sent(0)
        make_kept(0)
        relay(0)
        relay(1)
        scatter(0)
        relay(2)
        done([0, 2])
        make_sent(1)
        make_kept(1)
        relay(3)
        relay(5)
        relay(4)
        done([4, 5])
        make_sent(2)
        make_kept(2)
        spread(0)
        scatter(1)
        swap(0)
        scatter(2)
        spread(1)
        reflect()
        spread(2)
        swap(1)
        swap(3)
        place(0)
        swap(2)
        place(1)

    @pl.when(core == 1)
    def _():
        relay(0)
        relay(1)
        wait_other(0)
        make_sent(0)
        relay(2)
        done([0, 2])
        make_sent(1)
        relay(3)
        wait_other(1)
        make_kept(0)
        scatter(0)
        relay(5)
        make_kept(1)
        relay(4)
        done([4, 5])
        make_sent(2)
        make_kept(2)
        scatter(1)
        spread(0)
        scatter(2)
        spread(1)
        reflect()
        swap(0)
        spread(2)
        swap(1)
        swap(3)
        place(0)
        swap(2)
        place(1)

    done([1, 3])

    def send_partial(n, q):
        one = remote(
            part.at[n, q, 1], rbuf.at[n, q, core], ps.at[n, q, 1], pr.at[n, q, core],
            at(low_=other_low, core_=1),
        )
        one.start()

        @pl.when(core == 1)
        def _():
            remote(
                part.at[n, q, 0], rbuf.at[n, q, 1], ps.at[n, q, 0], pr.at[n, q, 1],
                at(low_=1 - low, core_=0),
            ).start()

    def reduced(n, q):
        remote(
            part.at[n, q, 1], rbuf.at[n, q, 1], ps.at[n, q, 1], pr.at[n, q, 1], twin
        ).wait_recv()

        @pl.when(core == 1)
        def _():
            remote(
                part.at[n, q, 0], rbuf.at[n, q, 0], ps.at[n, q, 0], pr.at[n, q, 0], twin
            ).wait_recv()

        @pl.when(core == 0)
        def _():
            rbuf[n, q, 0] = part[n, q, 0]

        return rbuf[n, q, 0].astype(F32) + rbuf[n, q, 1].astype(F32)

    def partial_close(n, q):
        remote(
            part.at[n, q, 1], rbuf.at[n, q, 1], ps.at[n, q, 1], pr.at[n, q, 1], twin
        ).wait_send()

        @pl.when(core == 1)
        def _():
            remote(
                part.at[n, q, 0], rbuf.at[n, q, 0], ps.at[n, q, 0], pr.at[n, q, 0], twin
            ).wait_send()

    def both(q, rows):
        cols = slice(q * Q, (q + 1) * Q)
        return jnp.concatenate([panel[0, rows, cols], panel[1, rows, cols]], axis=1)

    for q in range(NQ):
        yown[q] = jnp.dot(
            poly[:, 0 : 2 * S], both(q, slice(0, 2 * S)), preferred_element_type=F32
        )
    place(3)
    for q in range(NQ):
        yown[q] += jnp.dot(
            poly[:, 3 * S : 4 * S], both(q, slice(3 * S, 4 * S)), preferred_element_type=F32
        )
    place(2)
    for q in range(NQ):
        term = yown[q] + jnp.dot(
            poly[:, 2 * S : 3 * S], both(q, slice(2 * S, 3 * S)), preferred_element_type=F32
        )
        yown[q] = term
        for c in range(2):
            part[0, q, c] = term[:, c * Q : (c + 1) * Q].astype(BF16)
        send_partial(0, q)
    rings = []

    def begin(q):
        ypanel[q, core, pl.ds(0, B)] = reduced(0, q).astype(BF16)

        def yslot(c, at_row, rows):
            return ypanel.at[q, c, pl.ds(at_row, rows)]

        rings.append(gather(ypanel.at[q, core, pl.ds(0, B)], yslot, 1 + q))
        rings[q][0]()

    def finish(q):
        rings[q][2](range(7))
        both_y = jnp.concatenate([ypanel[q, 0], ypanel[q, 1]], axis=1)
        term = jnp.dot(poly[...], both_y, preferred_element_type=F32)
        term = 2.0315 * term - 4.775 * yown[q]
        for c in range(2):
            part[1, q, c] = term[:, c * Q : (c + 1) * Q].astype(BF16)
        send_partial(1, q)

    for t in range(NQ + 3):
        if t < NQ:
            begin(t)
        for back, ks in ((1, (0, 1)), (2, (2, 3)), (3, (4, 5))):
            if 0 <= t - back < NQ:
                for k in ks:
                    rings[t - back][1](k)
        if t >= 3:
            finish(t - 3)
    scale = math.sqrt(N)
    for q in range(NQ):
        cols = slice(q * Q, (q + 1) * Q)
        total = 3.4445 * x_ref[:, cols].astype(F32) + reduced(1, q)
        out_ref[:, cols] = (total * scale).astype(BF16)

    close()
    for k in range(2):
        other(k, core).wait_send()
    mirror.wait_send()
    for j in range(NJ):
        for c in [ysend[j]] + zsend[j]:
            c.wait_send()
    for j in range(NX):
        for c in hsend[j] + gsend[j]:
            c.wait_send()
    for q in range(NQ):
        rings[q][3]()
        for n in range(2):
            partial_close(n, q)


def on_device(iterate):
    dma = pltpu.SemaphoreType.DMA
    return pl.pallas_call(
        kernel,
        out_shape=jax.ShapeDtypeStruct((B, W), BF16),
        in_specs=[pl.BlockSpec(memory_space=pltpu.VMEM)],
        out_specs=pl.BlockSpec(memory_space=pltpu.VMEM),
        scratch_shapes=[
            pltpu.VMEM((2, NX * S + B, W), BF16),
            pltpu.VMEM((NQ, 2, NX * S, Q), BF16),
            pltpu.VMEM((NJ, HB, S), BF16),
            pltpu.VMEM((NJ, HB, S), F32),
            pltpu.VMEM((NJ, HB, S), BF16),
            pltpu.VMEM((NJ, 8, PR, PC), BF16),
            pltpu.VMEM((NJ, 7, PR, PC), BF16),
            pltpu.VMEM((NX, PR, PC), BF16),
            pltpu.VMEM((2, NX, 8, PR, PC), BF16),
            pltpu.VMEM((B, NX * S), BF16),
            pltpu.VMEM((B, S), F32),
            pltpu.VMEM((2, NQ, 2, B, Q), BF16),
            pltpu.VMEM((2, NQ, 2, B, Q), BF16),
            pltpu.VMEM((NQ, B, 2 * Q), F32),
            dma,
            dma((1 + NQ, 6)), dma((1 + NQ, 6)),
            dma((1 + NQ, 7)), dma((1 + NQ, 7)),
            dma((2,)), dma((2, 2)),
            dma((NJ,)), dma((NJ,)),
            dma((NJ, 7)), dma((NJ, 7)),
            dma((NX, 7)), dma((NX, 7)),
            dma((NX, 8)), dma((NX, 8)),
            dma((1,)), dma((1,)),
            dma((2, NQ, 2)), dma((2, NQ, 2)),
        ],
        compiler_params=pltpu.CompilerParams(
            collective_id=0, has_side_effects=True, vmem_limit_bytes=56 * 2**20
        ),
    )(iterate)


def solution(mesh):
    in_specs = (P("row", "col"),)
    out_specs = P("row", "col")
    return jax.shard_map(
        on_device, mesh=mesh, in_specs=in_specs, out_specs=out_specs, check_vma=False
    )
```

```python
import math

import jax
import jax.numpy as jnp
from jax import lax
from jax.experimental import pallas as pl
from jax.experimental.pallas import tpu as pltpu
from jax.sharding import PartitionSpec as P

N = 16384
B = 448
W = 512
S = 512
NX = 4
NJ = 3
NQ = 4
Q = W // NQ
HB = B // 2
PR = HB // 2
PC = S // 4
F32 = jnp.float32
BF16 = jnp.bfloat16
NT = (((1,), (1,)), ((), ()))
MESH = pl.DeviceIdType.MESH


def kernel(
    x_ref, out_ref, panel, ypanel, tsend, town, ybuf, zsrc, zbuf, gsh, agbuf, poly, mfull,
    part, rbuf, yown, loc_sem, xs, xr, cs, cr, ls, lr, ys, yr, zs, zr, gs, gr, hs, hr,
    ms, mr, ps, pr,
):
    row = lax.axis_index("row")
    col = lax.axis_index("col")
    x = row % 4
    low = row // 4
    core = col % 2
    high = (col // 2) % 2
    z = col // 4

    def at(x_=None, low_=None, z_=None, high_=None, core_=None):
        x_ = x if x_ is None else x_
        low_ = low if low_ is None else low_
        z_ = z if z_ is None else z_
        high_ = high if high_ is None else high_
        core_ = core if core_ is None else core_
        return (low_ * 4 + x_, z_ * 4 + high_ * 2 + core_)

    def remote(src, dst, send, recv, dev):
        return pltpu.make_async_remote_copy(
            src_ref=src, dst_ref=dst, send_sem=send, recv_sem=recv,
            device_id=dev, device_id_type=MESH,
        )

    pend = []
    up = at(x_=(x + 1) % 4)
    down = at(x_=(x + 3) % 4)
    twin = at(core_=1 - core)
    across = at(high_=1 - high)
    other_low = low + core * (1 - 2 * low)
    mirror_to = at(x_=(x + 1) % 4, low_=other_low)
    mirror_from = at(x_=(x + 3) % 4, low_=other_low)

    barrier = pltpu.get_barrier_semaphore()
    peers = [up, down, twin, across, mirror_to, mirror_from]
    peers += [at(low_=1 - low, core_=k) for k in range(2)]
    peers += [at(z_=(z + d) % 8) for d in range(1, 8)]
    for dev in peers:
        pl.semaphore_signal(barrier, inc=1, device_id=dev, device_id_type=MESH)
    for c in range(2):
        for j in range(NJ):
            panel[c, j * S + B : (j + 1) * S, :] = jnp.zeros((S - B, W), BF16)
    panel[0, 3 * S + B : 4 * S, :] = jnp.zeros((S - B, W), BF16)
    panel[1, 3 * S + B : 4 * S, :] = jnp.zeros((S - B, W), BF16)
    for q in range(NQ):
        for c in range(2):
            for j in range(NX):
                ypanel[q, c, j * S + B : (j + 1) * S, :] = jnp.zeros((S - B, Q), BF16)
    pl.semaphore_wait(barrier, len(peers))

    h = B // 2

    def gather(own, slot, n):
        a, b = pl.ds(0, h), pl.ds(h, h)
        direct = [
            remote(own.at[a], slot(core, S, h), xs.at[n, 0], xr.at[n, 0], down),
            remote(own.at[b], slot(core, 3 * S + h, h), xs.at[n, 1], xr.at[n, 1], up),
            remote(own.at[b], slot(core, S + h, h), xs.at[n, 2], xr.at[n, 2], down),
            remote(own.at[a], slot(core, 3 * S, h), xs.at[n, 3], xr.at[n, 3], up),
        ]
        passed = [
            remote(slot(core, S, h), slot(core, 2 * S, h), xs.at[n, 4], xr.at[n, 4], down),
            remote(slot(core, 3 * S + h, h), slot(core, 2 * S + h, h), xs.at[n, 5], xr.at[n, 5], up),
        ]
        moves = direct + passed
        places = [S, 3 * S + h, S + h, 3 * S, 2 * S, 2 * S + h]
        cross = [
            remote(slot(core, p, h), slot(core, p, h), cs.at[n, k], cr.at[n, k], twin)
            for k, p in enumerate(places)
        ]
        cross.append(remote(own, slot(core, 0, B), cs.at[n, 6], cr.at[n, 6], twin))

        def start():
            cross[6].start()
            for c in direct:
                c.start()

        def relay(k):
            moves[k].wait_recv()
            if k < 2:
                passed[k].start()
            cross[k].start()

        def done(ks):
            for k in ks:
                cross[k].wait_recv()

        def close():
            for c in moves + cross:
                c.wait_send()

        return start, relay, done, close

    def xslot(c, at_row, rows):
        return panel.at[c, pl.ds(at_row, rows)]

    start, relay, done, close = gather(x_ref, xslot, 0)
    start()
    def other(k, c):
        half = (1 - high) if k == 0 else high
        rows = pl.multiple_of(half * HB, 32)
        return remote(
            x_ref.at[pl.ds(rows, HB)], panel.at[c, pl.ds(NX * S + rows, HB)], ls.at[k],
            lr.at[k, c], at(low_=1 - low, core_=1),
        )

    for k in range(2):
        other(k, core).start()
    keep = pltpu.make_async_copy(x_ref, panel.at[core, pl.ds(0, B)], loc_sem)
    keep.start()
    keep.wait()
    done([6])

    left = core * NX * S

    def gram(half, j):
        rows = pl.ds(pl.multiple_of(left + half * HB, 32), HB)
        total = None
        for c in range(2):
            term = lax.dot_general(
                panel[c, rows, :], panel[c, pl.ds(j * S, S), :], NT, preferred_element_type=F32
            )
            total = term if total is None else total + term
        return total

    ysend = [remote(tsend.at[j], ybuf.at[j], ys.at[j], yr.at[j], across) for j in range(NJ)]

    def make_sent(j):
        tsend[j] = gram(1 - high, j).astype(BF16)
        ysend[j].start()

    def make_kept(j):
        town[j] = gram(high, j)

    zsend = [
        [
            remote(
                zsrc.at[j, (z + d) % 8], zbuf.at[j, d - 1], zs.at[j, d - 1], zr.at[j, d - 1],
                at(z_=(z + d) % 8),
            )
            for d in (4, 3, 5, 2, 6, 1, 7)
        ]
        for j in range(NJ)
    ]

    def scatter(j):
        ysend[j].wait_recv()
        for p in range(8):
            rows = slice(p % 2 * PR, (p % 2 + 1) * PR)
            cols = slice(p // 2 * PC, (p // 2 + 1) * PC)
            zsrc[j, p] = (town[j, rows, cols] + ybuf[j, rows, cols].astype(F32)).astype(BF16)
        for c in zsend[j]:
            c.start()

    def over_z(src, j, origin, d, to):
        dst = agbuf.at[high, j, origin % 8]
        return remote(src, dst, gs.at[j, d - 1], gr.at[j, d - 1], at(z_=to % 8))

    gsend = [
        [over_z(gsh.at[j], j, z, d, z + d) for d in (4, 3, 5, 2, 6, 1, 7)] for j in range(NX)
    ]

    def arrived(j, d):
        over_z(gsh.at[j], j, z + 8 - d, d, z + 1).wait_recv()

    def spread(j):
        total = zsrc[j, z].astype(F32)
        for c in zsend[j]:
            c.wait_recv()
        for k in range(7):
            total = total + zbuf[j, k].astype(F32)
        gsh[j] = total.astype(BF16)
        for c in gsend[j]:
            c.start()
        if j == 1:
            mirror.start()
        agbuf[high, j, z] = total.astype(BF16)
        hsend[j][0].start()

    hsend = [
        [
            remote(
                agbuf.at[high, j, (z + 8 - d) % 8], agbuf.at[high, j, (z + 8 - d) % 8],
                hs.at[j, d], hr.at[j, d], across,
            )
            for d in range(8)
        ]
        for j in range(NX)
    ]

    def swap(j):
        for d in (1, 7, 2, 6, 3, 5, 4):
            arrived(j, d)
            hsend[j][d].start()

    mirror = remote(gsh.at[1], gsh.at[3], ms.at[0], mr.at[0], mirror_to)

    def reflect():
        mirror.wait_recv()
        for c in gsend[3]:
            c.start()
        agbuf[high, 3, z] = gsh[3]
        hsend[3][0].start()

    def place(j):
        for c in hsend[j]:
            c.wait_recv()
        for half in range(2):
            for p in range(8):
                at_row = half * HB + p % 2 * PR
                at_col = p // 2 * PC
                if j == 3:
                    mfull[at_row : at_row + PR, at_col : at_col + PC] = agbuf[half, j, p].astype(F32)
                else:
                    at_col += j * S
                    poly[at_row : at_row + PR, at_col : at_col + PC] = agbuf[half, j, p]
        if j == 3:
            turned = mfull[...].T
            poly[:, 3 * S : 3 * S + B] = turned[0:B, :].astype(BF16)
            poly[:, 3 * S + B : 4 * S] = jnp.zeros((B, S - B), BF16)

    def wait_other(k):
        for c in range(2):
            other(k, c).wait_recv()

    @pl.when(core == 0)
    def _():
        make_sent(0)
        make_kept(0)
        relay(0)
        relay(1)
        scatter(0)
        relay(2)
        done([0, 2])
        make_sent(1)
        make_kept(1)
        relay(3)
        relay(5)
        relay(4)
        done([4, 5])
        make_sent(2)
        make_kept(2)
        spread(0)
        scatter(1)
        swap(0)
        scatter(2)
        spread(1)
        reflect()
        spread(2)
        swap(1)
        swap(3)
        place(0)
        swap(2)
        place(1)

    @pl.when(core == 1)
    def _():
        relay(0)
        relay(1)
        wait_other(0)
        make_sent(0)
        relay(2)
        done([0, 2])
        make_sent(1)
        relay(3)
        wait_other(1)
        make_kept(0)
        scatter(0)
        relay(5)
        make_kept(1)
        relay(4)
        done([4, 5])
        make_sent(2)
        make_kept(2)
        scatter(1)
        spread(0)
        scatter(2)
        spread(1)
        reflect()
        swap(0)
        spread(2)
        swap(1)
        swap(3)
        place(0)
        swap(2)
        place(1)

    done([1, 3])

    def send_partial(n, q):
        one = remote(
            part.at[n, q, 1], rbuf.at[n, q, core], ps.at[n, q, 1], pr.at[n, q, core],
            at(low_=other_low, core_=1),
        )
        one.start()

        @pl.when(core == 1)
        def _():
            remote(
                part.at[n, q, 0], rbuf.at[n, q, 1], ps.at[n, q, 0], pr.at[n, q, 1],
                at(low_=1 - low, core_=0),
            ).start()

    def reduced(n, q):
        remote(
            part.at[n, q, 1], rbuf.at[n, q, 1], ps.at[n, q, 1], pr.at[n, q, 1], twin
        ).wait_recv()

        @pl.when(core == 1)
        def _():
            remote(
                part.at[n, q, 0], rbuf.at[n, q, 0], ps.at[n, q, 0], pr.at[n, q, 0], twin
            ).wait_recv()

        @pl.when(core == 0)
        def _():
            rbuf[n, q, 0] = part[n, q, 0]

        return rbuf[n, q, 0].astype(F32) + rbuf[n, q, 1].astype(F32)

    def partial_close(n, q):
        remote(
            part.at[n, q, 1], rbuf.at[n, q, 1], ps.at[n, q, 1], pr.at[n, q, 1], twin
        ).wait_send()

        @pl.when(core == 1)
        def _():
            remote(
                part.at[n, q, 0], rbuf.at[n, q, 0], ps.at[n, q, 0], pr.at[n, q, 0], twin
            ).wait_send()

    def both(q, rows):
        cols = slice(q * Q, (q + 1) * Q)
        return jnp.concatenate([panel[0, rows, cols], panel[1, rows, cols]], axis=1)

    for q in range(NQ):
        yown[q] = jnp.dot(
            poly[:, 0 : 2 * S], both(q, slice(0, 2 * S)), preferred_element_type=F32
        )
    place(3)
    for q in range(NQ):
        yown[q] += jnp.dot(
            poly[:, 3 * S : 4 * S], both(q, slice(3 * S, 4 * S)), preferred_element_type=F32
        )
    place(2)
    for q in range(NQ):
        term = yown[q] + jnp.dot(
            poly[:, 2 * S : 3 * S], both(q, slice(2 * S, 3 * S)), preferred_element_type=F32
        )
        yown[q] = term
        for c in range(2):
            part[0, q, c] = term[:, c * Q : (c + 1) * Q].astype(BF16)
        send_partial(0, q)
    rings = []

    def begin(q):
        ypanel[q, core, pl.ds(0, B)] = reduced(0, q).astype(BF16)

        def yslot(c, at_row, rows):
            return ypanel.at[q, c, pl.ds(at_row, rows)]

        rings.append(gather(ypanel.at[q, core, pl.ds(0, B)], yslot, 1 + q))
        rings[q][0]()

    def finish(q):
        rings[q][2](range(7))
        both_y = jnp.concatenate([ypanel[q, 0], ypanel[q, 1]], axis=1)
        term = jnp.dot(poly[...], both_y, preferred_element_type=F32)
        term = 2.0315 * term - 4.775 * yown[q]
        for c in range(2):
            part[1, q, c] = term[:, c * Q : (c + 1) * Q].astype(BF16)
        send_partial(1, q)

    for t in range(NQ + 3):
        if t < NQ:
            begin(t)
        for back, ks in ((1, (0, 1)), (2, (2, 3)), (3, (4, 5))):
            if 0 <= t - back < NQ:
                for k in ks:
                    rings[t - back][1](k)
        if t >= 3:
            finish(t - 3)
    scale = math.sqrt(N)
    for q in range(NQ):
        cols = slice(q * Q, (q + 1) * Q)
        total = 3.4445 * x_ref[:, cols].astype(F32) + reduced(1, q)
        out_ref[:, cols] = (total * scale).astype(BF16)

    close()
    for k in range(2):
        other(k, core).wait_send()
    mirror.wait_send()
    for j in range(NJ):
        for c in [ysend[j]] + zsend[j]:
            c.wait_send()
    for j in range(NX):
        for c in hsend[j] + gsend[j]:
            c.wait_send()
    for q in range(NQ):
        rings[q][3]()
        for n in range(2):
            partial_close(n, q)


def on_device(iterate):
    dma = pltpu.SemaphoreType.DMA
    return pl.pallas_call(
        kernel,
        out_shape=jax.ShapeDtypeStruct((B, W), BF16),
        in_specs=[pl.BlockSpec(memory_space=pltpu.VMEM)],
        out_specs=pl.BlockSpec(memory_space=pltpu.VMEM),
        scratch_shapes=[
            pltpu.VMEM((2, NX * S + B, W), BF16),
            pltpu.VMEM((NQ, 2, NX * S, Q), BF16),
            pltpu.VMEM((NJ, HB, S), BF16),
            pltpu.VMEM((NJ, HB, S), F32),
            pltpu.VMEM((NJ, HB, S), BF16),
            pltpu.VMEM((NJ, 8, PR, PC), BF16),
            pltpu.VMEM((NJ, 7, PR, PC), BF16),
            pltpu.VMEM((NX, PR, PC), BF16),
            pltpu.VMEM((2, NX, 8, PR, PC), BF16),
            pltpu.VMEM((B, NX * S), BF16),
            pltpu.VMEM((B, S), F32),
            pltpu.VMEM((2, NQ, 2, B, Q), BF16),
            pltpu.VMEM((2, NQ, 2, B, Q), BF16),
            pltpu.VMEM((NQ, B, 2 * Q), F32),
            dma,
            dma((1 + NQ, 6)), dma((1 + NQ, 6)),
            dma((1 + NQ, 7)), dma((1 + NQ, 7)),
            dma((2,)), dma((2, 2)),
            dma((NJ,)), dma((NJ,)),
            dma((NJ, 7)), dma((NJ, 7)),
            dma((NX, 7)), dma((NX, 7)),
            dma((NX, 8)), dma((NX, 8)),
            dma((1,)), dma((1,)),
            dma((2, NQ, 2)), dma((2, NQ, 2)),
        ],
        compiler_params=pltpu.CompilerParams(
            collective_id=0, has_side_effects=True, vmem_limit_bytes=56 * 2**20
        ),
    )(iterate)


def solution(mesh):
    in_specs = (P("row", "col"),)
    out_specs = P("row", "col")
    return jax.shard_map(
        on_device, mesh=mesh, in_specs=in_specs, out_specs=out_specs, check_vma=False
    )
```
